32 devices in a mesh: parts: 2 (over x), cand: 16 (over z, y, core).
Axes of the slice: x: 2, y: 2, z: 4, core: 2. Of those that a mesh axis runs over, the one named last changes fastest.
Arguments:
- user_rows: bfloat16 [128, 16, 128], P(('parts', 'cand')), parts along dimension 0, may hold values from -6 to 6
- item_table: bfloat16 [8192, 512], P(('parts', 'cand')), parts along dimension 0, may hold values from -6 to 6
- cand_request: int32 [65536], P(('parts', 'cand')), parts along dimension 0, may hold values from 0 to 63, never falling along the last dimension, each value on 1 to 1000 neighbouring positions
- request_order: int32 [128], P('parts'), parts along dimension 0, may hold values from 0 to 63, as said below
- item_shard: int32 [65536, 1], P(('parts', 'cand')), parts along dimension 0, may hold values from 0 to 15; in each aligned block of 2048 rows (0 to 2047, 2048 to 4095, ...) at most 256 rows name the same one
- item_offset: int32 [65536], P(('parts', 'cand')), parts along dimension 0, may hold values from 0 to 255
- w_user: bfloat16 [256, 2048], replicated, may hold values from -0.375 to 0.375
- w_dots: bfloat16 [64, 2048], replicated, may hold values from -0.75 to 0.75
- w_item_gram: bfloat16 [16, 2048], replicated, may hold values from -1.5 to 1.5
- w_item: bfloat16 [512, 2048], replicated, may hold values from -0.25 to 0.25
- bias_one: bfloat16 [2048], replicated, may hold values from -3 to 3
- w_out: bfloat16 [2048], replicated, may hold values from -0.125 to 0.125
Outputs:
- scores: float32 [65536], P(('parts', 'cand')), parts along dimension 0
The draws below stay inside these ranges and needn't reach their ends.
There are 2 independent parts, one for each index of `parts`. The reference program is written for one: setup_inputs(seed, part) draws one part's arguments, and reference() takes and returns one part's arrays. A program takes and returns all parts, laid end to end along the dimension named above; an argument that names none is the same for every part. Nothing has to cross between parts.
Inputs may be any that keep to these rules, and one draw needn't show every extreme that they name: `cand_request`: never falls; each segment has 1 to 1000 candidates, one exactly 1000. `request_order`: a permutation of the requests. `item_shard`: among the candidates of one device at most 256 name one shard; some shard is named exactly 256 times by some device.
All inputs are finite; a program needn't handle non-finite values.
Results may differ from the reference program's by a relative error of at most 0.0035.
Values may be sent and summed in bfloat16 or wider, within the bound.
A program may use at most 128 MiB of HBM per device.

```python
import math
import jax
import jax.numpy as jnp
import numpy as np
from jax import lax

E = 128
NUF = 16
NIF = 4
H = 2048
MOSTC = 1000
ITEM_DEV = 256
CAND_DEV = 2048
REQ_DEV = 4
MOST = 256
REQ = 64
CANDS = 32768
ITEMS = 4096
N_CAND = 16


def draw_request_order(key, part):
    key = jax.random.fold_in(key, 7)
    shuffled = jax.random.permutation(key, REQ).astype(jnp.int32)
    target = jnp.int32(N_CAND // 2 * REQ_DEV)
    where_at = jnp.argmax(shuffled == target).astype(jnp.int32)
    leading = shuffled[0]
    shuffled = shuffled.at[where_at].set(leading)
    shuffled = shuffled.at[0].set(target)
    return shuffled


def with_ends(array, rng, low, top_value):
    shape = array.shape
    spot = [jax.random.randint(jax.random.fold_in(rng, axis), (), 0, shape[axis]) for axis in range(len(shape))]
    array = array.at[tuple(spot)].set(low)
    longest = shape.index(max(shape))
    spot[longest] = (spot[longest] + 1) % shape[longest]
    return array.at[tuple(spot)].set(top_value)


def block_scale(rng, extent, pieces, smallest, top_value):
    level = 1.0
    for axis_at, blocks in pieces:
        heights = jax.random.uniform(jax.random.fold_in(jax.random.fold_in(rng, 6), axis_at), (blocks,), jnp.float32, smallest / len(pieces), top_value / len(pieces))
        level = level * jnp.repeat(jnp.exp(heights), extent[axis_at] // blocks).reshape((-1,) + (1,) * (len(extent) - 1 - axis_at))
    return level


def profile(number_of, total, most, lean):
    loads = [(1 << 20) // math.isqrt(rank ** lean) + 1 for rank in range(2, number_of + 1)]
    rest, holding = total - most - (number_of - 1), [1] * (number_of - 1)
    while rest > 0:
        free = [i for i in range(number_of - 1) if holding[i] < most]
        mass, budget = sum([loads[i] for i in free]), rest
        for i in free:
            addition = min(most - holding[i], max(1, budget * loads[i] // mass), rest)
            holding[i] = holding[i] + addition
            rest = rest - addition
    return np.array([most] + holding)


def ragged(rng, number_of, total, reach, lean):
    if number_of == 2:
        one = jax.random.randint(rng, (), max(1, total - reach), min(reach, total - 1) + 1)
        return jnp.stack([one, total - one])
    tallies = jnp.asarray(profile(number_of, total, reach, lean), jnp.int32)
    couples = (number_of - 1) // 2
    donor, receiver = tallies[1:1 + 2 * couples:2], tallies[2:2 + 2 * couples:2]
    margin = jnp.minimum(donor - 1, reach - receiver)
    moved = jax.random.randint(jax.random.fold_in(rng, 1), (couples,), 0, 1 << 20) % (margin + 1)
    tallies = tallies.at[1:1 + 2 * couples:2].set(donor - moved).at[2:2 + 2 * couples:2].set(receiver + moved)
    return tallies[jax.random.permutation(jax.random.fold_in(rng, 2), number_of)]


def shared_out(own_key, own, number, rows, amount, top, reach, slope):
    sequence = jax.random.permutation(own_key, amount)
    heavy_load, usual = shares(amount, rows * top, reach, slope, True), shares(amount, rows * top, reach, slope, False)
    places = jnp.arange(amount)

    def named(sizes, offset_by):
        used = int((sizes > 0).sum())
        fixed = max(1, used // 4)
        shifted = fixed + (places - fixed + offset_by * (used - fixed)) % max(1, amount - fixed)
        return jnp.zeros((amount,), jnp.int32).at[sequence[jnp.where(places < fixed, places, shifted)]].set(jnp.asarray(sizes, jnp.int32))

    sizes = jnp.where(number % 4 == 0, named(heavy_load, number // 4), named(usual, number - number // 4 - 1))
    mixed = jax.random.permutation(jax.random.fold_in(own, 3), amount)
    giver, receiver = mixed[0:amount // 2 * 2:2], mixed[1:amount // 2 * 2:2]
    margin = jnp.minimum(sizes[giver] - 1, reach - sizes[receiver]) // 2
    margin = jnp.where((giver == sequence[0]) | (receiver == sequence[0]) | (sizes[receiver] == 0), 0, jnp.maximum(margin, 0))
    shifted = jax.random.randint(jax.random.fold_in(own, 4), (amount // 2,), 0, 1 << 20) % (margin + 1)
    sizes = sizes.at[giver].add(-shifted).at[receiver].add(shifted)
    labels = jnp.searchsorted(jnp.cumsum(sizes), jnp.arange(rows * top), side="right").astype(jnp.int32)
    listing = labels.reshape(top, rows).T
    listing = listing[jax.random.permutation(jax.random.fold_in(own, 1), rows)]
    offset_by = jax.random.randint(jax.random.fold_in(own, 2), (rows, 1), 0, top)
    return jnp.take_along_axis(listing, (jnp.arange(top)[None, :] + offset_by) % top, axis=1)


def shares(number_of, total, bound, skew, full):
    portions = [(1 << 20) // math.isqrt(standing ** skew) + 1 for standing in range(1, number_of + 1)]
    largest = bound if full else min(bound, max(-(-total // number_of), total * portions[0] // sum(portions)))
    least = 1 if total - largest >= number_of - 1 else 0
    counts, surplus = [largest] + [least] * (number_of - 1), total - largest - least * (number_of - 1)
    while surplus > 0:
        candidates = [i for i in range(1, number_of) if counts[i] < largest] or [i for i in range(1, number_of) if counts[i] < bound]
        pool, remaining = sum([portions[i] for i in candidates]), surplus
        for i in candidates:
            more = min(bound - counts[i], max(1, remaining * portions[i] // pool), surplus)
            counts[i] = counts[i] + more
            surplus = surplus - more
    return np.array(counts)


def centred(own_key, extent, scale, bound, cuts=(), held_as=jnp.bfloat16):
    array = jax.random.normal(own_key, extent, jnp.float32) * scale
    if len(cuts) > 0:
        array = block_scale(own_key, extent, cuts, -0.22, 0.18) * array
    return jnp.clip(array, min=-bound, max=bound).astype(held_as)


def setup_inputs(seed: int = 0, part: int = 0) -> dict:
    splits = jax.random.split(jax.random.key(seed), 13)
    own_keys = jax.random.split(jax.random.fold_in(splits[12], part), 13)
    user_rows = centred(own_keys[0], (REQ, NUF, E), 1.0, 6.0, ((0, 16),))
    item_table = centred(own_keys[1], (ITEMS, NIF * E), 1.0, 6.0, ((0, 16),))
    cand_request = jnp.searchsorted(jnp.cumsum(ragged(own_keys[2], REQ, CANDS, MOSTC, 2)), jnp.arange(CANDS), side="right").astype(jnp.int32)
    request_order = draw_request_order(jax.random.fold_in(jax.random.fold_in(splits[12], part), 71), part)
    item_shard_keys = jax.random.split(jax.random.fold_in(own_keys[4], 1), CANDS // CAND_DEV)
    item_shard_turns = jax.random.permutation(jax.random.fold_in(own_keys[4], 3), CANDS // CAND_DEV)
    item_shard = jax.vmap(lambda own, number: shared_out(jax.random.fold_in(own_keys[4], 2), own, number, CAND_DEV, N_CAND, 1, MOST, 2))(item_shard_keys, item_shard_turns).reshape((CANDS, 1))
    item_offset = with_ends(jax.random.randint(own_keys[5], (CANDS,), 0, ITEM_DEV), jax.random.fold_in(own_keys[5], 1), 0, ITEM_DEV - 1).astype(jnp.int32)
    w_user = centred(splits[6], (NUF * NUF, H), (NUF * NUF) ** -0.5, 0.375)
    w_dots = centred(splits[7], (NUF * NIF, H), (NUF * NIF) ** -0.5, 0.75)
    w_item_gram = centred(splits[8], (NIF * NIF, H), (NIF * NIF) ** -0.5, 1.5)
    w_item = centred(splits[9], (NIF * E, H), (NIF * E) ** -0.5, 0.25)
    bias_one = centred(splits[10], (H,), 0.5, 3.0)
    w_out = centred(splits[11], (H,), H ** -0.5, 0.125)
    return {"user_rows": user_rows, "item_table": item_table, "cand_request": cand_request, "request_order": request_order, "item_shard": item_shard, "item_offset": item_offset, "w_user": w_user, "w_dots": w_dots, "w_item_gram": w_item_gram, "w_item": w_item, "bias_one": bias_one, "w_out": w_out}


def reference(user_rows, item_table, cand_request, request_order, item_shard, item_offset, w_user, w_dots, w_item_gram, w_item, bias_one, w_out):
    user_f32 = user_rows.astype(jnp.float32)
    user_gram = (jnp.einsum('rue,rve->ruv', user_f32, user_f32) / E).astype(jnp.bfloat16)
    user_term = jnp.dot(user_gram.reshape(REQ, NUF * NUF), w_user, preferred_element_type=jnp.float32).astype(jnp.bfloat16)
    flat_users = user_rows.reshape(REQ, NUF * E)
    cand_req = jnp.take(request_order, cand_request, axis=0).astype(jnp.int32)
    row_index = (item_shard[:, 0] * ITEM_DEV + item_offset).astype(jnp.int32)

    def scores_of(inputs):
        requests, rows_at = inputs
        picked = flat_users[requests].reshape(-1, NUF, E).astype(jnp.float32)
        items = item_table[rows_at]
        items_three = items.reshape(-1, NIF, E).astype(jnp.float32)
        dots = (jnp.einsum('cue,cie->cui', picked, items_three) / math.sqrt(E)).astype(jnp.bfloat16).reshape(-1, NUF * NIF)
        item_gram = (jnp.einsum('cie,cje->cij', items_three, items_three) / E).astype(jnp.bfloat16).reshape(-1, NIF * NIF)
        preact = user_term[requests].astype(jnp.float32)
        preact = preact + jnp.dot(dots, w_dots, preferred_element_type=jnp.float32)
        preact = preact + jnp.dot(item_gram, w_item_gram, preferred_element_type=jnp.float32)
        preact = preact + jnp.dot(items, w_item, preferred_element_type=jnp.float32)
        preact = preact + bias_one.astype(jnp.float32)
        hidden = jax.nn.relu(preact).astype(jnp.bfloat16)
        return jnp.dot(hidden, w_out, preferred_element_type=jnp.float32)
    blocks = lax.map(scores_of, (cand_req.reshape(-1, CAND_DEV), row_index.reshape(-1, CAND_DEV)))
    return blocks.reshape(CANDS)
```

```python
import functools
import math

import jax
import jax.numpy as jnp
from jax import lax
from jax.experimental import pallas as pl
from jax.experimental.pallas import tpu as pltpu
from jax.sharding import PartitionSpec as P

BF16 = jnp.bfloat16
F32 = jnp.float32
I32 = jnp.int32


def iota(shape, dim):
    return lax.broadcasted_iota(I32, shape, dim)


def onehot(mask):
    return jnp.where(mask, F32(1), F32(0)).astype(BF16)


def kernel(
    dims,
    users_hbm,
    table_hbm,
    seg_ref,
    order_ref,
    shard_ref,
    offset_ref,
    w_user_hbm,
    w_dots_ref,
    w_gram_ref,
    w_item_hbm,
    bias_ref,
    w_out_ref,
    out_ref,
    buf,
    xt,
    wt,
    wut,
    w_item,
    w_user,
    w_tail,
    tt,
    users,
    gram_t,
    wout_b,
    rid,
    req,
    load_sem,
    send_sem,
    recv_sem,
):
    nz, ny, req_dev, feats, width, nif, item_dev, cands, hidden = dims
    nreq = nz * ny * 2 * req_dev
    row = nif * width
    per_slot = req_dev * feats
    piece = per_slot // nif
    shift = feats.bit_length() - 1
    me = lax.axis_index("cand")
    core = me % 2
    y = (me // 2) % ny
    z = me // (2 * ny)

    def index(zz, yy, cc):
        return (zz * ny + yy) * 2 + cc

    up, down = index(z + 1, y, core), index(z - 1, y, core)
    across, beside = index(z, ny - 1 - y, core), index(z, y, 1 - core)

    loads = []
    for i in range(nif):
        loads.append(
            pltpu.make_async_copy(
                table_hbm.at[:, pl.ds(i * width, width)],
                buf.at[me, i, pl.ds(0, item_dev)],
                load_sem.at[2 * i],
            )
        )
        loads.append(
            pltpu.make_async_copy(
                users_hbm.at[pl.ds(i * piece, piece)],
                buf.at[me, i, pl.ds(item_dev, piece)],
                load_sem.at[2 * i + 1],
            )
        )
    for load in loads:
        load.start()
    get_item = pltpu.make_async_copy(w_item_hbm, w_item, load_sem.at[2 * nif])
    get_user = pltpu.make_async_copy(w_user_hbm, w_user, load_sem.at[2 * nif + 1])
    get_item.start()
    get_user.start()

    barrier = pltpu.get_barrier_semaphore()

    def near(device, exists):
        @pl.when(exists)
        def _():
            pl.semaphore_signal(
                barrier, inc=1, device_id={"cand": device}, device_id_type=pl.DeviceIdType.MESH
            )

    always = z >= 0
    near(up, z + 1 < nz)
    near(down, z > 0)
    if ny == 2:
        near(across, always)
    near(beside, always)
    peers = ny + (z + 1 < nz).astype(I32) + (z > 0).astype(I32)
    pl.semaphore_wait(barrier, peers)

    def copy(slot, way, device):
        return pltpu.make_async_remote_copy(
            src_ref=buf.at[slot],
            dst_ref=buf.at[slot],
            send_sem=send_sem.at[way, slot],
            recv_sem=recv_sem.at[slot],
            device_id={"cand": device},
            device_id_type=pl.DeviceIdType.MESH,
        )

    def await_slot(slot):
        copy(slot, 0, beside).wait_recv()

    for load in loads:
        load.wait()

    @pl.when(z + 1 < nz)
    def _():
        copy(me, 0, up).start()

    @pl.when(z > 0)
    def _():
        copy(me, 1, down).start()

    if ny == 2:
        copy(me, 2, across).start()
    copy(me, 3, beside).start()

    xt[...] = jnp.zeros_like(xt)
    gram_t[...] = jnp.zeros_like(gram_t)
    rid[...] = shard_ref[...] * item_dev + offset_ref[...]
    seg = seg_ref[...]
    req[...] = lax.fori_loop(
        0,
        nreq,
        lambda s, total: total + jnp.where(seg == s, order_ref[s], 0),
        jnp.zeros_like(seg),
    )
    nd, ng = feats * nif, nif * nif
    turn = onehot(
        iota((nd, nd), 1) == (iota((nd, nd), 0) & (feats - 1)) * nif + (iota((nd, nd), 0) >> shift)
    )
    w_tail[...] = jnp.zeros_like(w_tail)
    w_tail[0:nd] = jnp.dot(turn, w_dots_ref[...], preferred_element_type=F32).astype(BF16)
    w_tail[nd : nd + ng] = w_gram_ref[...]
    bias_row = jnp.broadcast_to(bias_ref[...].astype(F32), (16, hidden))
    w_tail[nd + ng : nd + ng + 16] = jnp.where(iota((16, hidden), 0) == 0, bias_row, 0.0).astype(
        BF16
    )
    base = w_tail.shape[0]
    step_h = 256

    get_item.wait()
    get_user.wait()

    @pl.loop(0, hidden // step_h)
    def _(h):
        at = pl.ds(pl.multiple_of(h * step_h, step_h), step_h)
        wt[at, 0:row] = w_item[:, at].T
        wt[at, row : row + base] = w_tail[:, at].T
        wut[at, :] = w_user[:, at].T
        wout_b[at, :] = jnp.broadcast_to(w_out_ref[:, at].astype(F32), (128, step_h)).T

    pair_rows = 2 * item_dev
    block = 512
    nu = 2 * per_slot
    nf = feats * feats

    def take_in(zz, yy, exists):
        @pl.when(exists)
        def _():
            first = index(zz, yy, 0)
            await_slot(first + 1 - core)
            for lane in range(2):
                for i in range(nif):
                    tt[i * width : (i + 1) * width, lane * item_dev : (lane + 1) * item_dev] = buf[
                        first + lane, i, 0:item_dev, :
                    ].T

            @pl.loop(0, cands // block)
            def _(n):
                at = pl.ds(pl.multiple_of(n * block, block), block)
                hit = onehot(rid[:, at] - first * item_dev == iota((pair_rows, block), 0))
                xt[0:row, at] += jnp.dot(tt[...], hit, preferred_element_type=F32).astype(BF16)

            here = buf[pl.ds(first, 2), :, item_dev : item_dev + piece, :].reshape(nu, width)
            users[pl.ds(pl.multiple_of(first * per_slot, nu), nu), :] = here
            gram = lax.dot_general(
                here, here, (((1,), (1,)), ((), ())), preferred_element_type=F32
            ) * F32(1 / width)
            same = (iota((nu, nu), 0) >> shift) == (iota((nu, nu), 1) >> shift)
            gram = jnp.where(same, gram, 0.0).astype(BF16)
            spread = onehot((iota((nf, nu), 0) >> shift) == (iota((nf, nu), 1) & (feats - 1)))
            wide = jnp.dot(spread, gram, preferred_element_type=F32)
            keep = (iota((nf, nu), 0) & (feats - 1)) == (iota((nf, nu), 1) & (feats - 1))
            wide = jnp.where(keep, wide, 0.0).astype(BF16)
            place = onehot(
                iota((nu, nreq), 1) == first * req_dev + (iota((nu, nreq), 0) >> shift)
            )
            gram_t[...] += jnp.dot(wide, place, preferred_element_type=F32)

    @pl.loop(1, nz + 2)
    def _(t):
        later = t < nz
        low, high = z - t, z + t

        @pl.when(later & (low >= 0))
        def _():
            slot = index(low, y, core)
            await_slot(slot)

            @pl.when(z + 1 < nz)
            def _():
                copy(slot, 0, up).start()

            if ny == 2:
                copy(slot, 2, across).start()
            copy(slot, 3, beside).start()

        @pl.when(later & (high < nz))
        def _():
            slot = index(high, y, core)
            await_slot(slot)

            @pl.when(z > 0)
            def _():
                copy(slot, 1, down).start()

            if ny == 2:
                copy(slot, 2, across).start()
            copy(slot, 3, beside).start()

        a, b = z - (t - 1), z + (t - 1)
        has_a, has_b = (a >= 0) & (t <= nz), (b < nz) & (t >= 2) & (t <= nz)
        if ny == 2:
            for zz, has in ((a, has_a), (b, has_b)):

                @pl.when(has)
                def _(zz=zz):
                    slot = index(zz, 1 - y, core)
                    await_slot(slot)
                    copy(slot, 3, beside).start()

        take_in(a, y, has_a)
        take_in(b, y, has_b)
        if ny == 2:
            c, d = z - (t - 2), z + (t - 2)
            take_in(c, 1 - y, (c >= 0) & (t >= 2))
            take_in(d, 1 - y, (d < nz) & (t >= 3))

    term_at = row + base

    @pl.loop(0, hidden // step_h)
    def _(h):
        at = pl.ds(pl.multiple_of(h * step_h, step_h), step_h)
        wt[at, term_at : term_at + nreq] = jnp.dot(
            wut[at, :], gram_t[...].astype(BF16), preferred_element_type=F32
        ).astype(BF16)

    span = 256

    @pl.loop(0, cands // span)
    def _(n):
        at = pl.ds(pl.multiple_of(n * span, span), span)
        who = req[:, at]
        group = 16
        vectors = []
        for i in range(nif):
            item = xt[i * width : (i + 1) * width, at]
            total = jnp.zeros((feats, span), F32)
            for g in range(nreq // group):
                rows = group * feats
                z_all = jnp.dot(
                    users[g * rows : (g + 1) * rows, :], item, preferred_element_type=F32
                ).reshape(group, feats, span)
                hit = (who == iota((group, span), 0) + g * group)[:, None, :]
                total = total + jnp.sum(jnp.where(hit, z_all, 0.0), axis=0)
            xt[row + i * feats : row + (i + 1) * feats, at] = (
                total * F32(1 / math.sqrt(width))
            ).astype(BF16)
            vectors.append(item.astype(F32))
        grams = {}
        for i in range(nif):
            for j in range(i, nif):
                grams[i, j] = grams[j, i] = jnp.sum(
                    vectors[i] * vectors[j], axis=0, keepdims=True
                )
        gram_rows = jnp.concatenate(
            [grams[i, j] for i in range(nif) for j in range(nif)], axis=0
        ) * F32(1 / width)
        xt[row + nd : row + nd + ng, at] = gram_rows.astype(BF16)
        xt[row + nd + ng : row + nd + ng + 16, at] = onehot(iota((16, span), 0) == 0)
        xt[term_at : term_at + nreq, at] = onehot(who == iota((nreq, span), 0))
        x = xt[:, at]
        score = jnp.zeros((8, span), F32)
        for h in range(hidden // step_h):
            pre = jnp.dot(
                wt[h * step_h : (h + 1) * step_h, :], x, preferred_element_type=F32
            )
            w = wout_b[h * step_h : (h + 1) * step_h, :]
            act = jnp.maximum(pre, 0.0) * jnp.concatenate([w] * (span // 128), axis=1)
            score = score + jnp.sum(act.reshape(step_h // 8, 8, span), axis=0)
        out_ref[:, at] = jnp.sum(score, axis=0, keepdims=True)

    @pl.when(z + 1 < nz)
    def _():
        @pl.loop(0, nz)
        def _(zz):
            @pl.when(zz <= z)
            def _():
                copy(index(zz, y, core), 0, up).wait_send()

    @pl.when(z > 0)
    def _():
        @pl.loop(0, nz)
        def _(zz):
            @pl.when(zz >= z)
            def _():
                copy(index(zz, y, core), 1, down).wait_send()

    @pl.loop(0, nz)
    def _(zz):
        if ny == 2:
            copy(index(zz, y, core), 2, across).wait_send()
        for yy in range(ny):
            copy(index(zz, yy, core), 3, beside).wait_send()


def shards(
    ny,
    user_rows,
    item_table,
    cand_request,
    request_order,
    item_shard,
    item_offset,
    w_user,
    w_dots,
    w_item_gram,
    w_item,
    bias_one,
    w_out,
):
    req_dev, feats, width = user_rows.shape
    item_dev, row = item_table.shape
    nif = row // width
    cands = cand_request.shape[0]
    hidden = w_out.shape[0]
    num = lax.axis_size("cand")
    nz = num // (2 * ny)
    nreq = num * req_dev
    base = -(-(feats * nif + nif * nif + 16) // 128) * 128
    depth = row + base + -(-nreq // 128) * 128
    slot_rows = item_dev + req_dev * feats // nif
    vmem = pl.BlockSpec(memory_space=pltpu.VMEM)
    smem = pl.BlockSpec(memory_space=pltpu.SMEM)
    hbm = pl.BlockSpec(memory_space=pl.ANY)
    dims = (nz, ny, req_dev, feats, width, nif, item_dev, cands, hidden)
    scores = pl.pallas_call(
        functools.partial(kernel, dims),
        out_shape=jax.ShapeDtypeStruct((1, cands), F32),
        in_specs=[hbm, hbm, vmem, smem, vmem, vmem, hbm, vmem, vmem, hbm, vmem, vmem],
        out_specs=vmem,
        scratch_shapes=[
            pltpu.VMEM((num, nif, slot_rows, width), BF16),
            pltpu.VMEM((depth, cands), BF16),
            pltpu.VMEM((hidden, depth), BF16),
            pltpu.VMEM((hidden, feats * feats), BF16),
            pltpu.VMEM((row, hidden), BF16),
            pltpu.VMEM((feats * feats, hidden), BF16),
            pltpu.VMEM((base, hidden), BF16),
            pltpu.VMEM((row, 2 * item_dev), BF16),
            pltpu.VMEM((nreq * feats, width), BF16),
            pltpu.VMEM((feats * feats, nreq), F32),
            pltpu.VMEM((hidden, 128), F32),
            pltpu.VMEM((1, cands), I32),
            pltpu.VMEM((1, cands), I32),
            pltpu.SemaphoreType.DMA((2 * nif + 2,)),
            pltpu.SemaphoreType.DMA((4, num)),
            pltpu.SemaphoreType.DMA((num,)),
        ],
        compiler_params=pltpu.CompilerParams(
            collective_id=0, has_side_effects=True, vmem_limit_bytes=56 * 1024 * 1024
        ),
        cost_estimate=pl.CostEstimate(
            flops=2 * cands * hidden * depth, bytes_accessed=8 << 20, transcendentals=0
        ),
    )(
        user_rows.reshape(req_dev * feats, width),
        item_table,
        cand_request.reshape(1, cands),
        request_order,
        item_shard.reshape(1, cands),
        item_offset.reshape(1, cands),
        w_user,
        w_dots,
        w_item_gram,
        w_item,
        bias_one.reshape(1, hidden),
        w_out.reshape(1, hidden),
    )
    return scores.reshape(cands)


def solution(mesh):
    ny = 4 // mesh.shape["parts"]
    in_specs = (
        P(("parts", "cand"), None, None),
        P(("parts", "cand"), None),
        P(("parts", "cand")),
        P("parts"),
        P(("parts", "cand"), None),
        P(("parts", "cand")),
        P(),
        P(),
        P(),
        P(),
        P(),
        P(),
    )
    out_specs = P(("parts", "cand"))
    return jax.shard_map(
        functools.partial(shards, ny),
        mesh=mesh,
        in_specs=in_specs,
        out_specs=out_specs,
        check_vma=False,
    )
```

```python
import functools
import math

import jax
import jax.numpy as jnp
from jax import lax
from jax.experimental import pallas as pl
from jax.experimental.pallas import tpu as pltpu
from jax.sharding import PartitionSpec as P

BF16 = jnp.bfloat16
F32 = jnp.float32
I32 = jnp.int32


def iota(shape, dim):
    return lax.broadcasted_iota(I32, shape, dim)


def onehot(mask):
    return jnp.where(mask, F32(1), F32(0)).astype(BF16)


def kernel(
    dims,
    users_hbm,
    table_hbm,
    seg_ref,
    order_ref,
    shard_ref,
    offset_ref,
    w_user_hbm,
    w_dots_ref,
    w_gram_ref,
    w_item_hbm,
    bias_ref,
    w_out_ref,
    out_ref,
    buf,
    xt,
    wt,
    wut,
    w_item,
    w_user,
    w_tail,
    tt,
    users,
    gram_t,
    wout_b,
    rid,
    req,
    load_sem,
    send_sem,
    recv_sem,
):
    nz, ny, req_dev, feats, width, nif, item_dev, cands, hidden = dims
    nreq = nz * ny * 2 * req_dev
    row = nif * width
    per_slot = req_dev * feats
    piece = per_slot // nif
    shift = feats.bit_length() - 1
    me = lax.axis_index("cand")
    core = me % 2
    y = (me // 2) % ny
    z = me // (2 * ny)

    def index(zz, yy, cc):
        return (zz * ny + yy) * 2 + cc

    up, down = index(z + 1, y, core), index(z - 1, y, core)
    across, beside = index(z, ny - 1 - y, core), index(z, y, 1 - core)

    loads = []
    for i in range(nif):
        loads.append(
            pltpu.make_async_copy(
                table_hbm.at[:, pl.ds(i * width, width)],
                buf.at[me, i, pl.ds(0, item_dev)],
                load_sem.at[2 * i],
            )
        )
        loads.append(
            pltpu.make_async_copy(
                users_hbm.at[pl.ds(i * piece, piece)],
                buf.at[me, i, pl.ds(item_dev, piece)],
                load_sem.at[2 * i + 1],
            )
        )
    for load in loads:
        load.start()
    get_item = pltpu.make_async_copy(w_item_hbm, w_item, load_sem.at[2 * nif])
    get_user = pltpu.make_async_copy(w_user_hbm, w_user, load_sem.at[2 * nif + 1])
    get_item.start()
    get_user.start()

    barrier = pltpu.get_barrier_semaphore()

    def near(device, exists):
        @pl.when(exists)
        def _():
            pl.semaphore_signal(
                barrier, inc=1, device_id={"cand": device}, device_id_type=pl.DeviceIdType.MESH
            )

    always = z >= 0
    near(up, z + 1 < nz)
    near(down, z > 0)
    if ny == 2:
        near(across, always)
    near(beside, always)
    peers = ny + (z + 1 < nz).astype(I32) + (z > 0).astype(I32)
    pl.semaphore_wait(barrier, peers)

    balanced = ny == 2 and nz >= 4
    part = nif // 2

    def copy(slot, half, way, device):
        return pltpu.make_async_remote_copy(
            src_ref=buf.at[slot, pl.ds(half * part, part)],
            dst_ref=buf.at[slot, pl.ds(half * part, part)],
            send_sem=send_sem.at[way, slot, half],
            recv_sem=recv_sem.at[slot, half],
            device_id={"cand": device},
            device_id_type=pl.DeviceIdType.MESH,
        )

    def await_half(slot, half):
        copy(slot, half, 0, beside).wait_recv()

    def forward(zz, own_column, half, act):
        slot = index(zz, y if own_column else 1 - y, core)
        if own_column:
            go_up, go_down, go_across = zz <= z, zz >= z, None
            if balanced:
                by_z = ((z == 1) & (zz == 0)) | ((z == nz - 2) & (zz == nz - 1))
                if half == 1:
                    by_z |= ((z == 0) & (zz == nz - 1)) | ((z == nz - 1) & (zz == 0))
                go_across = jnp.logical_not(by_z)
            elif ny == 2:
                go_across = always
        else:
            go_up = go_down = go_across = None
            if balanced:
                go_up, go_down = (z == 0) & (zz == 0), (z == nz - 1) & (zz == nz - 1)
                if half == 1:
                    go_up |= (z == nz - 2) & (zz == 0)
                    go_down |= (z == 1) & (zz == nz - 1)
        for way, device, go in (
            (0, up, None if go_up is None else go_up & (z + 1 < nz)),
            (1, down, None if go_down is None else go_down & (z > 0)),
            (2, across, go_across),
            (3, beside, always),
        ):
            if go is not None:

                @pl.when(go)
                def _(way=way, device=device):
                    act(copy(slot, half, way, device))

    def start(c):
        c.start()

    def finish(c):
        c.wait_send()

    for load in loads:
        load.wait()

    for half in range(2):
        forward(z, True, half, start)

    xt[...] = jnp.zeros_like(xt)
    gram_t[...] = jnp.zeros_like(gram_t)
    rid[...] = shard_ref[...] * item_dev + offset_ref[...]
    seg = seg_ref[...]
    req[...] = lax.fori_loop(
        0,
        nreq,
        lambda s, total: total + jnp.where(seg == s, order_ref[s], 0),
        jnp.zeros_like(seg),
    )
    nd, ng = feats * nif, nif * nif
    turn = onehot(
        iota((nd, nd), 1) == (iota((nd, nd), 0) & (feats - 1)) * nif + (iota((nd, nd), 0) >> shift)
    )
    w_tail[...] = jnp.zeros_like(w_tail)
    w_tail[0:nd] = jnp.dot(turn, w_dots_ref[...], preferred_element_type=F32).astype(BF16)
    w_tail[nd : nd + ng] = w_gram_ref[...]
    bias_row = jnp.broadcast_to(bias_ref[...].astype(F32).reshape(1, hidden), (16, hidden))
    w_tail[nd + ng : nd + ng + 16] = jnp.where(iota((16, hidden), 0) == 0, bias_row, 0.0).astype(
        BF16
    )
    base = w_tail.shape[0]
    step_h = 256

    get_item.wait()
    get_user.wait()

    @pl.loop(0, hidden // step_h)
    def _(h):
        at = pl.ds(pl.multiple_of(h * step_h, step_h), step_h)
        wt[at, 0:row] = w_item[:, at].T
        wt[at, row : row + base] = w_tail[:, at].T
        wut[at, :] = w_user[:, at].T
        wout_b[at, :] = jnp.broadcast_to(w_out_ref[at].astype(F32).reshape(1, step_h), (128, step_h)).T

    pair_rows = 2 * item_dev
    block = 512
    nu = 2 * per_slot
    nf = feats * feats

    def take_in(zz, yy, exists):
        @pl.when(exists)
        def _():
            first = index(zz, yy, 0)
            for half in range(2):
                await_half(first + 1 - core, half)
            for lane in range(2):
                for i in range(nif):
                    tt[i * width : (i + 1) * width, lane * item_dev : (lane + 1) * item_dev] = buf[
                        first + lane, i, 0:item_dev, :
                    ].T

            rows_t = tt[...]
            for n in range(cands // block):
                at = pl.ds(n * block, block)
                hit = onehot(rid[:, at] - first * item_dev == iota((pair_rows, block), 0))
                xt[0:row, at] += jnp.dot(rows_t, hit, preferred_element_type=F32).astype(BF16)

            here = buf[pl.ds(first, 2), :, item_dev : item_dev + piece, :].reshape(nu, width)
            users[pl.ds(pl.multiple_of(first * per_slot, nu), nu), :] = here
            gram = lax.dot_general(
                here, here, (((1,), (1,)), ((), ())), preferred_element_type=F32
            ) * F32(1 / width)
            same = (iota((nu, nu), 0) >> shift) == (iota((nu, nu), 1) >> shift)
            gram = jnp.where(same, gram, 0.0).astype(BF16)
            spread = onehot((iota((nf, nu), 0) >> shift) == (iota((nf, nu), 1) & (feats - 1)))
            wide = jnp.dot(spread, gram, preferred_element_type=F32)
            keep = (iota((nf, nu), 0) & (feats - 1)) == (iota((nf, nu), 1) & (feats - 1))
            wide = jnp.where(keep, wide, 0.0).astype(BF16)
            place = onehot(
                iota((nu, nreq), 1) == first * req_dev + (iota((nu, nreq), 0) >> shift)
            )
            gram_t[...] += jnp.dot(wide, place, preferred_element_type=F32)

    def relay(zz, own_column, half, exists):
        @pl.when(exists)
        def _():
            await_half(index(zz, y if own_column else 1 - y, core), half)
            forward(zz, own_column, half, start)

    @pl.loop(1, nz + 2)
    def _(t):
        a, b = z - (t - 1), z + (t - 1)
        has_a, has_b = (a >= 0) & (t <= nz), (b < nz) & (t >= 2) & (t <= nz)
        c, d = z - (t - 2), z + (t - 2)
        for half in range(2):
            relay(z - t, True, half, (t < nz) & (z - t >= 0))
            relay(z + t, True, half, (t < nz) & (z + t < nz))
            if ny == 2:
                relay(a, False, half, has_a)
                relay(b, False, half, has_b)
            if half == 0:
                take_in(a, y, has_a)
                take_in(b, y, has_b)
            elif ny == 2:
                take_in(c, 1 - y, (c >= 0) & (t >= 2))
                take_in(d, 1 - y, (d < nz) & (t >= 3))

    term_at = row + base

    @pl.loop(0, hidden // step_h)
    def _(h):
        at = pl.ds(pl.multiple_of(h * step_h, step_h), step_h)
        wt[at, term_at : term_at + nreq] = jnp.dot(
            wut[at, :], gram_t[...].astype(BF16), preferred_element_type=F32
        ).astype(BF16)

    span = 256

    @pl.loop(0, cands // span, unroll=2)
    def _(n):
        at = pl.ds(pl.multiple_of(n * span, span), span)
        who = req[:, at]
        group = 16
        vectors = []
        for i in range(nif):
            item = xt[i * width : (i + 1) * width, at]
            total = jnp.zeros((feats, span), F32)
            for g in range(nreq // group):
                rows = group * feats
                z_all = jnp.dot(
                    users[g * rows : (g + 1) * rows, :], item, preferred_element_type=F32
                ).reshape(group, feats, span)
                hit = (who == iota((group, span), 0) + g * group)[:, None, :]
                total = total + jnp.sum(jnp.where(hit, z_all, 0.0), axis=0)
            xt[row + i * feats : row + (i + 1) * feats, at] = (
                total * F32(1 / math.sqrt(width))
            ).astype(BF16)
            vectors.append(item.astype(F32))
        grams = {}
        for i in range(nif):
            for j in range(i, nif):
                grams[i, j] = grams[j, i] = jnp.sum(
                    vectors[i] * vectors[j], axis=0, keepdims=True
                )
        gram_rows = jnp.concatenate(
            [grams[i, j] for i in range(nif) for j in range(nif)], axis=0
        ) * F32(1 / width)
        xt[row + nd : row + nd + ng, at] = gram_rows.astype(BF16)
        xt[row + nd + ng : row + nd + ng + 16, at] = onehot(iota((16, span), 0) == 0)
        xt[term_at : term_at + nreq, at] = onehot(who == iota((nreq, span), 0))
        x = xt[:, at]
        score = jnp.zeros((8, span), F32)
        for h in range(hidden // step_h):
            pre = jnp.dot(
                wt[h * step_h : (h + 1) * step_h, :], x, preferred_element_type=F32
            )
            w = wout_b[h * step_h : (h + 1) * step_h, :]
            act = jnp.maximum(pre, 0.0) * jnp.concatenate([w] * (span // 128), axis=1)
            score = score + jnp.sum(act.reshape(step_h // 8, 8, span), axis=0)
        out_ref[:, at] = jnp.sum(score, axis=0, keepdims=True)

    @pl.loop(0, nz)
    def _(zz):
        for half in range(2):
            forward(zz, True, half, finish)
            if ny == 2:
                forward(zz, False, half, finish)


def shards(
    ny,
    user_rows,
    item_table,
    cand_request,
    request_order,
    item_shard,
    item_offset,
    w_user,
    w_dots,
    w_item_gram,
    w_item,
    bias_one,
    w_out,
):
    req_dev, feats, width = user_rows.shape
    item_dev, row = item_table.shape
    nif = row // width
    cands = cand_request.shape[0]
    hidden = w_out.shape[0]
    num = lax.axis_size("cand")
    nz = num // (2 * ny)
    nreq = num * req_dev
    base = -(-(feats * nif + nif * nif + 16) // 128) * 128
    depth = row + base + -(-nreq // 128) * 128
    slot_rows = item_dev + req_dev * feats // nif
    vmem = pl.BlockSpec(memory_space=pltpu.VMEM)
    smem = pl.BlockSpec(memory_space=pltpu.SMEM)
    hbm = pl.BlockSpec(memory_space=pl.ANY)
    dims = (nz, ny, req_dev, feats, width, nif, item_dev, cands, hidden)
    scores = pl.pallas_call(
        functools.partial(kernel, dims),
        out_shape=jax.ShapeDtypeStruct((1, cands), F32),
        in_specs=[hbm, hbm, vmem, smem, vmem, vmem, hbm, vmem, vmem, hbm, vmem, vmem],
        out_specs=vmem,
        scratch_shapes=[
            pltpu.VMEM((num, nif, slot_rows, width), BF16),
            pltpu.VMEM((depth, cands), BF16),
            pltpu.VMEM((hidden, depth), BF16),
            pltpu.VMEM((hidden, feats * feats), BF16),
            pltpu.VMEM((row, hidden), BF16),
            pltpu.VMEM((feats * feats, hidden), BF16),
            pltpu.VMEM((base, hidden), BF16),
            pltpu.VMEM((row, 2 * item_dev), BF16),
            pltpu.VMEM((nreq * feats, width), BF16),
            pltpu.VMEM((feats * feats, nreq), F32),
            pltpu.VMEM((hidden, 128), F32),
            pltpu.VMEM((1, cands), I32),
            pltpu.VMEM((1, cands), I32),
            pltpu.SemaphoreType.DMA((2 * nif + 2,)),
            pltpu.SemaphoreType.DMA((4, num, 2)),
            pltpu.SemaphoreType.DMA((num, 2)),
        ],
        compiler_params=pltpu.CompilerParams(
            collective_id=0, has_side_effects=True, vmem_limit_bytes=56 * 1024 * 1024
        ),
        cost_estimate=pl.CostEstimate(
            flops=2 * cands * hidden * depth, bytes_accessed=8 << 20, transcendentals=0
        ),
    )(
        user_rows.reshape(req_dev * feats, width),
        item_table,
        cand_request.reshape(1, cands),
        request_order,
        item_shard.reshape(1, cands),
        item_offset.reshape(1, cands),
        w_user,
        w_dots,
        w_item_gram,
        w_item,
        bias_one,
        w_out,
    )
    return scores.reshape(cands)


def solution(mesh):
    ny = 4 // mesh.shape["parts"]
    in_specs = (
        P(("parts", "cand"), None, None),
        P(("parts", "cand"), None),
        P(("parts", "cand")),
        P("parts"),
        P(("parts", "cand"), None),
        P(("parts", "cand")),
        P(),
        P(),
        P(),
        P(),
        P(),
        P(),
    )
    out_specs = P(("parts", "cand"))
    return jax.shard_map(
        functools.partial(shards, ny),
        mesh=mesh,
        in_specs=in_specs,
        out_specs=out_specs,
        check_vma=False,
    )
```

```python
import functools
import math

import jax
import jax.numpy as jnp
from jax import lax
from jax.experimental import pallas as pl
from jax.experimental.pallas import tpu as pltpu
from jax.sharding import PartitionSpec as P

BF16 = jnp.bfloat16
F32 = jnp.float32
I32 = jnp.int32


def iota(shape, dim):
    return lax.broadcasted_iota(I32, shape, dim)


def onehot(mask):
    return jnp.where(mask, F32(1), F32(0)).astype(BF16)


def kernel(
    dims,
    users_hbm,
    table_hbm,
    seg_hbm,
    order_ref,
    shard_hbm,
    offset_hbm,
    w_user_hbm,
    w_dots_hbm,
    w_gram_hbm,
    w_item_hbm,
    bias_hbm,
    w_out_hbm,
    out_ref,
    buf,
    xt,
    wt,
    wut,
    w_item,
    w_user,
    w_tail,
    tt,
    users,
    gram_t,
    wout_b,
    rid,
    req,
    seg_ref,
    shard_ref,
    offset_ref,
    w_dots_ref,
    w_gram_ref,
    bias_ref,
    w_out_ref,
    load_sem,
    send_sem,
    recv_sem,
):
    nz, ny, req_dev, feats, width, nif, item_dev, cands, hidden = dims
    nreq = nz * ny * 2 * req_dev
    row = nif * width
    per_slot = req_dev * feats
    piece = per_slot // nif
    shift = feats.bit_length() - 1
    me = lax.axis_index("cand")
    core = me % 2
    y = (me // 2) % ny
    z = me // (2 * ny)

    def index(zz, yy, cc):
        return (zz * ny + yy) * 2 + cc

    up, down = index(z + 1, y, core), index(z - 1, y, core)
    across, beside = index(z, ny - 1 - y, core), index(z, y, 1 - core)

    loads = []
    for i in range(nif):
        loads.append(
            pltpu.make_async_copy(
                table_hbm.at[:, pl.ds(i * width, width)],
                buf.at[me, i, pl.ds(0, item_dev)],
                load_sem.at[2 * i],
            )
        )
        loads.append(
            pltpu.make_async_copy(
                users_hbm.at[pl.ds(i * piece, piece)],
                buf.at[me, i, pl.ds(item_dev, piece)],
                load_sem.at[2 * i + 1],
            )
        )
    for load in loads:
        load.start()
    get_item = pltpu.make_async_copy(w_item_hbm, w_item, load_sem.at[2 * nif])
    get_user = pltpu.make_async_copy(w_user_hbm, w_user, load_sem.at[2 * nif + 1])
    get_item.start()
    get_user.start()
    small = []
    for k, (source, target) in enumerate(
        (
            (seg_hbm, seg_ref),
            (shard_hbm, shard_ref),
            (offset_hbm, offset_ref),
            (w_dots_hbm, w_dots_ref),
            (w_gram_hbm, w_gram_ref),
            (bias_hbm, bias_ref),
            (w_out_hbm, w_out_ref),
        )
    ):
        small.append(pltpu.make_async_copy(source, target, load_sem.at[2 * nif + 2 + k]))
    for load in small:
        load.start()

    barrier = pltpu.get_barrier_semaphore()

    def near(device, exists):
        @pl.when(exists)
        def _():
            pl.semaphore_signal(
                barrier, inc=1, device_id={"cand": device}, device_id_type=pl.DeviceIdType.MESH
            )

    always = z >= 0
    near(up, z + 1 < nz)
    near(down, z > 0)
    if ny == 2:
        near(across, always)
    near(beside, always)
    peers = ny + (z + 1 < nz).astype(I32) + (z > 0).astype(I32)
    pl.semaphore_wait(barrier, peers)

    balanced = ny == 2 and nz >= 4
    part = nif // 2

    def copy(slot, half, way, device):
        return pltpu.make_async_remote_copy(
            src_ref=buf.at[slot, pl.ds(half * part, part)],
            dst_ref=buf.at[slot, pl.ds(half * part, part)],
            send_sem=send_sem.at[way, slot, half],
            recv_sem=recv_sem.at[slot, half],
            device_id={"cand": device},
            device_id_type=pl.DeviceIdType.MESH,
        )

    def await_half(slot, half):
        copy(slot, half, 0, beside).wait_recv()

    def forward(zz, own_column, half, act):
        slot = index(zz, y if own_column else 1 - y, core)
        if own_column:
            go_up, go_down, go_across = zz <= z, zz >= z, None
            if balanced:
                by_z = ((z == 1) & (zz == 0)) | ((z == nz - 2) & (zz == nz - 1))
                if half == 1:
                    by_z |= ((z == 0) & (zz == nz - 1)) | ((z == nz - 1) & (zz == 0))
                go_across = jnp.logical_not(by_z)
            elif ny == 2:
                go_across = always
        else:
            go_up = go_down = go_across = None
            if balanced:
                go_up, go_down = (z == 0) & (zz == 0), (z == nz - 1) & (zz == nz - 1)
                if half == 1:
                    go_up |= (z == nz - 2) & (zz == 0)
                    go_down |= (z == 1) & (zz == nz - 1)
        for way, device, go in (
            (0, up, None if go_up is None else go_up & (z + 1 < nz)),
            (1, down, None if go_down is None else go_down & (z > 0)),
            (2, across, go_across),
            (3, beside, always),
        ):
            if go is not None:

                @pl.when(go)
                def _(way=way, device=device):
                    act(copy(slot, half, way, device))

    def start(c):
        c.start()

    def finish(c):
        c.wait_send()

    for half in range(2):
        for load in loads[half * nif : (half + 1) * nif]:
            load.wait()
        forward(z, True, half, start)

    for load in small:
        load.wait()

    xt[...] = jnp.zeros_like(xt)
    gram_t[...] = jnp.zeros_like(gram_t)
    rid[...] = shard_ref[...] * item_dev + offset_ref[...]
    seg = seg_ref[...]
    req[...] = lax.fori_loop(
        0,
        nreq,
        lambda s, total: total + jnp.where(seg == s, order_ref[s], 0),
        jnp.zeros_like(seg),
    )
    nd, ng = feats * nif, nif * nif
    turn = onehot(
        iota((nd, nd), 1) == (iota((nd, nd), 0) & (feats - 1)) * nif + (iota((nd, nd), 0) >> shift)
    )
    w_tail[...] = jnp.zeros_like(w_tail)
    w_tail[0:nd] = jnp.dot(turn, w_dots_ref[...], preferred_element_type=F32).astype(BF16)
    w_tail[nd : nd + ng] = w_gram_ref[...]
    bias_row = jnp.broadcast_to(bias_ref[...].astype(F32).reshape(1, hidden), (16, hidden))
    w_tail[nd + ng : nd + ng + 16] = jnp.where(iota((16, hidden), 0) == 0, bias_row, 0.0).astype(
        BF16
    )
    base = w_tail.shape[0]
    step_h = 256

    get_item.wait()
    get_user.wait()

    @pl.loop(0, hidden // step_h)
    def _(h):
        at = pl.ds(pl.multiple_of(h * step_h, step_h), step_h)
        wt[at, 0:row] = w_item[:, at].T
        wt[at, row : row + base] = w_tail[:, at].T
        wut[at, :] = w_user[:, at].T
        wout_b[at, :] = jnp.broadcast_to(w_out_ref[at].astype(F32).reshape(1, step_h), (128, step_h)).T

    pair_rows = 2 * item_dev
    block = 512
    nu = 2 * per_slot
    nf = feats * feats

    def take_in(zz, yy, exists):
        @pl.when(exists)
        def _():
            first = index(zz, yy, 0)
            for half in range(2):
                await_half(first + 1 - core, half)
            for lane in range(2):
                for i in range(nif):
                    tt[i * width : (i + 1) * width, lane * item_dev : (lane + 1) * item_dev] = buf[
                        first + lane, i, 0:item_dev, :
                    ].T

            rows_t = tt[...]
            for n in range(cands // block):
                at = pl.ds(n * block, block)
                hit = onehot(rid[:, at] - first * item_dev == iota((pair_rows, block), 0))
                xt[0:row, at] += jnp.dot(rows_t, hit, preferred_element_type=F32).astype(BF16)

            here = buf[pl.ds(first, 2), :, item_dev : item_dev + piece, :].reshape(nu, width)
            users[pl.ds(pl.multiple_of(first * per_slot, nu), nu), :] = here
            gram = lax.dot_general(
                here, here, (((1,), (1,)), ((), ())), preferred_element_type=F32
            ) * F32(1 / width)
            same = (iota((nu, nu), 0) >> shift) == (iota((nu, nu), 1) >> shift)
            gram = jnp.where(same, gram, 0.0).astype(BF16)
            spread = onehot((iota((nf, nu), 0) >> shift) == (iota((nf, nu), 1) & (feats - 1)))
            wide = jnp.dot(spread, gram, preferred_element_type=F32)
            keep = (iota((nf, nu), 0) & (feats - 1)) == (iota((nf, nu), 1) & (feats - 1))
            wide = jnp.where(keep, wide, 0.0).astype(BF16)
            place = onehot(
                iota((nu, nreq), 1) == first * req_dev + (iota((nu, nreq), 0) >> shift)
            )
            gram_t[...] += jnp.dot(wide, place, preferred_element_type=F32)

    def relay(zz, own_column, half, exists):
        @pl.when(exists)
        def _():
            await_half(index(zz, y if own_column else 1 - y, core), half)
            forward(zz, own_column, half, start)

    @pl.loop(1, nz + 2)
    def _(t):
        a, b = z - (t - 1), z + (t - 1)
        has_a, has_b = (a >= 0) & (t <= nz), (b < nz) & (t >= 2) & (t <= nz)
        c, d = z - (t - 2), z + (t - 2)
        for half in range(2):
            relay(z - t, True, half, (t < nz) & (z - t >= 0))
            relay(z + t, True, half, (t < nz) & (z + t < nz))
            if ny == 2:
                relay(a, False, half, has_a)
                relay(b, False, half, has_b)
            if half == 0:
                take_in(a, y, has_a)
                take_in(b, y, has_b)
            elif ny == 2:
                take_in(c, 1 - y, (c >= 0) & (t >= 2))
                take_in(d, 1 - y, (d < nz) & (t >= 3))

    term_at = row + base

    @pl.loop(0, hidden // step_h)
    def _(h):
        at = pl.ds(pl.multiple_of(h * step_h, step_h), step_h)
        wt[at, term_at : term_at + nreq] = jnp.dot(
            wut[at, :], gram_t[...].astype(BF16), preferred_element_type=F32
        ).astype(BF16)

    span = 512

    @pl.loop(0, cands // span, unroll=2)
    def _(n):
        at = pl.ds(pl.multiple_of(n * span, span), span)
        who = req[:, at]
        group = 16
        vectors = []
        for i in range(nif):
            item = xt[i * width : (i + 1) * width, at]
            total = jnp.zeros((feats, span), F32)
            for g in range(nreq // group):
                rows = group * feats
                z_all = jnp.dot(
                    users[g * rows : (g + 1) * rows, :], item, preferred_element_type=F32
                ).reshape(group, feats, span)
                hit = (who == iota((group, span), 0) + g * group)[:, None, :]
                total = total + jnp.sum(jnp.where(hit, z_all, 0.0), axis=0)
            xt[row + i * feats : row + (i + 1) * feats, at] = (
                total * F32(1 / math.sqrt(width))
            ).astype(BF16)
            vectors.append(item.astype(F32))
        grams = {}
        for i in range(nif):
            for j in range(i, nif):
                grams[i, j] = grams[j, i] = jnp.sum(
                    vectors[i] * vectors[j], axis=0, keepdims=True
                )
        gram_rows = jnp.concatenate(
            [grams[i, j] for i in range(nif) for j in range(nif)], axis=0
        ) * F32(1 / width)
        xt[row + nd : row + nd + ng, at] = gram_rows.astype(BF16)
        xt[row + nd + ng : row + nd + ng + 16, at] = onehot(iota((16, span), 0) == 0)
        xt[term_at : term_at + nreq, at] = onehot(who == iota((nreq, span), 0))
        x = xt[:, at]
        score = jnp.zeros((8, span), F32)
        for h in range(hidden // step_h):
            pre = jnp.dot(
                wt[h * step_h : (h + 1) * step_h, :], x, preferred_element_type=F32
            )
            w = wout_b[h * step_h : (h + 1) * step_h, :]
            act = jnp.maximum(pre, 0.0) * jnp.concatenate([w] * (span // 128), axis=1)
            score = score + jnp.sum(act.reshape(step_h // 8, 8, span), axis=0)
        out_ref[:, at] = jnp.sum(score, axis=0, keepdims=True)

    @pl.loop(0, nz)
    def _(zz):
        for half in range(2):
            forward(zz, True, half, finish)
            if ny == 2:
                forward(zz, False, half, finish)


def shards(
    ny,
    user_rows,
    item_table,
    cand_request,
    request_order,
    item_shard,
    item_offset,
    w_user,
    w_dots,
    w_item_gram,
    w_item,
    bias_one,
    w_out,
):
    req_dev, feats, width = user_rows.shape
    item_dev, row = item_table.shape
    nif = row // width
    cands = cand_request.shape[0]
    hidden = w_out.shape[0]
    num = lax.axis_size("cand")
    nz = num // (2 * ny)
    nreq = num * req_dev
    base = -(-(feats * nif + nif * nif + 16) // 128) * 128
    depth = row + base + -(-nreq // 128) * 128
    slot_rows = item_dev + req_dev * feats // nif
    vmem = pl.BlockSpec(memory_space=pltpu.VMEM)
    smem = pl.BlockSpec(memory_space=pltpu.SMEM)
    hbm = pl.BlockSpec(memory_space=pl.ANY)
    dims = (nz, ny, req_dev, feats, width, nif, item_dev, cands, hidden)
    scores = pl.pallas_call(
        functools.partial(kernel, dims),
        out_shape=jax.ShapeDtypeStruct((1, cands), F32),
        in_specs=[hbm] * 3 + [smem] + [hbm] * 8,
        out_specs=vmem,
        scratch_shapes=[
            pltpu.VMEM((num, nif, slot_rows, width), BF16),
            pltpu.VMEM((depth, cands), BF16),
            pltpu.VMEM((hidden, depth), BF16),
            pltpu.VMEM((hidden, feats * feats), BF16),
            pltpu.VMEM((row, hidden), BF16),
            pltpu.VMEM((feats * feats, hidden), BF16),
            pltpu.VMEM((base, hidden), BF16),
            pltpu.VMEM((row, 2 * item_dev), BF16),
            pltpu.VMEM((nreq * feats, width), BF16),
            pltpu.VMEM((feats * feats, nreq), F32),
            pltpu.VMEM((hidden, 128), F32),
            pltpu.VMEM((1, cands), I32),
            pltpu.VMEM((1, cands), I32),
            pltpu.VMEM((1, cands), I32),
            pltpu.VMEM((1, cands), I32),
            pltpu.VMEM((1, cands), I32),
            pltpu.VMEM(w_dots.shape, BF16),
            pltpu.VMEM(w_item_gram.shape, BF16),
            pltpu.VMEM(bias_one.shape, BF16),
            pltpu.VMEM(w_out.shape, BF16),
            pltpu.SemaphoreType.DMA((2 * nif + 9,)),
            pltpu.SemaphoreType.DMA((4, num, 2)),
            pltpu.SemaphoreType.DMA((num, 2)),
        ],
        compiler_params=pltpu.CompilerParams(
            collective_id=0, has_side_effects=True, vmem_limit_bytes=56 * 1024 * 1024
        ),
        cost_estimate=pl.CostEstimate(
            flops=2 * cands * hidden * depth, bytes_accessed=8 << 20, transcendentals=0
        ),
    )(
        user_rows.reshape(req_dev * feats, width),
        item_table,
        cand_request.reshape(1, cands),
        request_order,
        item_shard.reshape(1, cands),
        item_offset.reshape(1, cands),
        w_user,
        w_dots,
        w_item_gram,
        w_item,
        bias_one,
        w_out,
    )
    return scores.reshape(cands)


def solution(mesh):
    ny = 4 // mesh.shape["parts"]
    in_specs = (
        P(("parts", "cand"), None, None),
        P(("parts", "cand"), None),
        P(("parts", "cand")),
        P("parts"),
        P(("parts", "cand"), None),
        P(("parts", "cand")),
        P(),
        P(),
        P(),
        P(),
        P(),
        P(),
    )
    out_specs = P(("parts", "cand"))
    return jax.shard_map(
        functools.partial(shards, ny),
        mesh=mesh,
        in_specs=in_specs,
        out_specs=out_specs,
        check_vma=False,
    )
```
